256 devices in a mesh: span: 8 (over x, core), ulysses: 32 (over z, y).
Axes of the slice: x: 4, y: 4, z: 8, core: 2. Of those that a mesh axis runs over, the one named last changes fastest.
Arguments:
- query: bfloat16 [8, 1536, 4096], P('span', 'ulysses'), may hold values from -5 to 5
- keys_in: bfloat16 [8, 1536, 4096], P('span', 'ulysses'), may hold values from -5 to 5
- values_in: bfloat16 [8, 1536, 4096], P('span', 'ulysses'), may hold values from -6 to 6
- out_weight: bfloat16 [4096, 6144], P('ulysses'), may hold values from -0.75 to 0.75
- gate_table: bfloat16 [64, 6144], replicated, may hold values from 0.5 to 2
- levels: int32 [8], replicated, may hold values from 0 to 63
- first_visible: int32 [8], replicated, may hold values from 0 to 3, as said below
Outputs:
- update: bfloat16 [8, 1536, 6144], P('span', 'ulysses')
The draws below stay inside these ranges and needn't reach their ends.
Inputs may be any that keep to these rules, and one draw needn't show every extreme that they name: first_visible[c] is at most c // 2 for span c; for the last span, whose index c is 7, it equals c // 2 exactly.
All inputs are finite; a program needn't handle non-finite values.
Results may differ from the reference program's by a relative error of at most 0.025.
Values may be sent and summed in bfloat16 or wider, within the bound.
A program may use at most 128 MiB of HBM per device.

```python
import jax
import jax.numpy as jnp
from jax import lax

D = 6144
HEADS = 32
HD = 128
LEVELS = 64
SPANS = 8
SPAN_TOK = 1536
N_ULYSSES = 32


def draw_query(key, part):
    shape = (SPANS, SPAN_TOK, HEADS * HD)
    key = jax.random.fold_in(key, 1)
    values = jnp.clip(1.5 * jax.random.normal(key, shape, jnp.float32), -5.0, 5.0)
    return values.astype(jnp.bfloat16)


def draw_keys_in(key, part):
    shape = (SPANS, SPAN_TOK, HEADS * HD)
    key = jax.random.fold_in(key, 2)
    values = jnp.clip(jax.random.normal(key, shape, jnp.float32), -5.0, 5.0)
    return values.astype(jnp.bfloat16)


def draw_first_visible(key, part):
    key = jax.random.fold_in(key, 3)
    index = jnp.arange(SPANS, dtype=jnp.int32)
    raw = jax.random.randint(key, (SPANS,), 0, 1 << 20, dtype=jnp.int32)
    drawn = (raw % (index // 2 + 1)).astype(jnp.int32)
    return jnp.where(index == SPANS - 1, index // 2, drawn).astype(jnp.int32)


def set_ends(values, key, least, largest):
    longest = values.shape.index(max(values.shape))
    spots = []
    for shift in (0, 1):
        where = [jax.random.randint(jax.random.fold_in(key, axis), (), 0, length) for axis, length in enumerate(values.shape)]
        where[longest] = (where[longest] + shift) % values.shape[longest]
        spots.append(tuple(where))
    return values.at[spots[0]].set(least).at[spots[1]].set(largest)


def block_scale(rng, dims, shards, low, top_value):
    def one(position, shards_of):
        heights = jax.random.uniform(jax.random.fold_in(jax.random.fold_in(rng, 6), position), (shards_of,), jnp.float32, low / len(shards), top_value / len(shards))
        return jnp.repeat(jnp.exp(heights), dims[position] // shards_of).reshape((-1,) + (1,) * (len(dims) - position - 1))

    level = one(*shards[0])
    for cut in shards[1:]:
        level = level * one(*cut)
    return level


def scatter_about(stream_key, shape, scale, bound, split=(), kind=jnp.bfloat16):
    values = scale * jax.random.normal(stream_key, shape, jnp.float32)
    if split:
        values = values * block_scale(stream_key, shape, split, -0.22, 0.18)
    return jnp.clip(values, -bound, bound).astype(kind)


def setup_inputs(seed: int = 0) -> dict:
    streams_of = jax.random.split(jax.random.key(seed), 8)
    query = draw_query(jax.random.fold_in(streams_of[7], 71), 0)
    keys_in = draw_keys_in(jax.random.fold_in(streams_of[7], 71), 0)
    values_in = scatter_about(streams_of[2], (SPANS, SPAN_TOK, HEADS * HD), 1.0, 6.0, ((0, 8), (1, 32)))
    out_weight = scatter_about(streams_of[3], (HEADS * HD, D), 0.125, 0.75, ((0, 32),))
    gate_table = jnp.clip(jax.random.uniform(streams_of[4], (LEVELS, D), jnp.float32, 0.5, 2.0), 0.5, 2.0).astype(jnp.bfloat16)
    levels = set_ends(jax.random.randint(streams_of[5], (SPANS,), 0, LEVELS), jax.random.fold_in(streams_of[5], 1), 0, LEVELS - 1).astype(jnp.int32)
    first_visible = draw_first_visible(jax.random.fold_in(streams_of[7], 71), 0)
    return {"query": query, "keys_in": keys_in, "values_in": values_in, "out_weight": out_weight, "gate_table": gate_table, "levels": levels, "first_visible": first_visible}


def span_attention(query_rows, keys_all, values_all, visible):
    scale = 1.0 / (HD ** 0.5)

    def one_head(operands):
        q_head, k_head, v_head = operands
        scores = jnp.dot(q_head, k_head.T, preferred_element_type=jnp.float32) * scale
        masked = jnp.where(visible[None, :], scores, -jnp.inf)
        top = jnp.max(masked, axis=1, keepdims=True)
        expo = jnp.where(visible[None, :], jnp.exp(scores - top), jnp.float32(0.0))
        total = jnp.sum(expo, axis=1, keepdims=True)
        probs = expo.astype(jnp.bfloat16)
        summed = jnp.dot(probs, v_head, preferred_element_type=jnp.float32)
        return (summed / total).astype(jnp.bfloat16)

    return lax.map(one_head, (query_rows, keys_all, values_all))


def reference(query, keys_in, values_in, out_weight, gate_table, levels, first_visible):
    span_tok = query.shape[1]
    width = HEADS * HD
    groups = N_ULYSSES
    group_width = width // groups
    keys_all = keys_in.reshape(SPANS * span_tok, HEADS, HD).transpose(1, 0, 2)
    values_all = values_in.reshape(SPANS * span_tok, HEADS, HD).transpose(1, 0, 2)
    key_span = jnp.arange(SPANS * span_tok, dtype=jnp.int32) // span_tok
    weight_groups = out_weight.reshape(groups, group_width, D)
    outputs = []
    for span_now in range(SPANS):
        visible = (key_span >= first_visible[span_now]) & (key_span <= span_now)
        query_rows = query[span_now].reshape(span_tok, HEADS, HD).transpose(1, 0, 2)
        attn = span_attention(query_rows, keys_all, values_all, visible)
        attn = attn.transpose(1, 0, 2).reshape(span_tok, groups, group_width)

        def add_group(total, index):
            part_attn = lax.dynamic_index_in_dim(attn, index, 1, keepdims=False)
            part_weight = lax.dynamic_index_in_dim(weight_groups, index, 0, keepdims=False)
            partial_value = jnp.dot(part_attn, part_weight, preferred_element_type=jnp.float32).astype(jnp.bfloat16)
            partial_value = lax.optimization_barrier(partial_value)
            return total + partial_value.astype(jnp.float32), None

        projected, _ = lax.scan(add_group, jnp.zeros((span_tok, D), jnp.float32), jnp.arange(groups, dtype=jnp.int32))
        gate = gate_table[levels[span_now]].astype(jnp.float32)
        outputs.append((gate[None, :] * projected).astype(jnp.bfloat16))
    return jnp.stack(outputs, axis=0)
```

```python
import functools
import math

import jax
import jax.numpy as jnp
from jax import lax
from jax.experimental import pallas as pl
from jax.experimental.pallas import tpu as pltpu
from jax.sharding import PartitionSpec as P

MESH = pl.DeviceIdType.MESH
f32, bf16 = jnp.float32, jnp.bfloat16

HD = 128
TOK = 1536
OWN = 48
Z, Y, X = 8, 4, 4
SLAB = 192
WIDE = 6144
COLS = WIDE // 8
HALF = 768
KC = 512
C = math.log2(math.e) / math.sqrt(HD)
LOW = -1e30


def remote(src, dst, send_sem, recv_sem, device):
    return pltpu.make_async_remote_copy(
        src_ref=src, dst_ref=dst, send_sem=send_sem, recv_sem=recv_sem, device_id=device, device_id_type=MESH
    )


def wait_bytes(ref, sem):
    pltpu.make_async_copy(ref, ref, sem).wait()


def kernel(
    q_in, k_in, v_in, w_in, gate_in, levels, first, out,
    qb, kb, vb, vt, po_s, po_r, ob, ag, wf, pb, rb,
    a2a_s, a2a_r, kx_s, kx_r, vx_s, vx_r, qx_s, qx_r, po_ss, po_rs, oz_s, oz_r, ag_s, ag_r, w_s, w_r, w_l, y_s, y_r,
):
    s, u = lax.axis_index("span"), lax.axis_index("ulysses")
    x, k = s // 2, s % 2
    z, y = u // Y, u % Y
    sib = x * 2 + (1 - k)

    barrier = pltpu.get_barrier_semaphore()

    def hail_ulysses(d, c):
        pl.semaphore_signal(barrier, inc=1, device_id=(s, (u + d) % 32), device_id_type=MESH)
        return c

    def hail_plane(d, c):
        pl.semaphore_signal(
            barrier, inc=1, device_id=((s + 1 + d // Y) % 8, z * Y + d % Y), device_id_type=MESH
        )
        return c

    lax.fori_loop(1, 32, hail_ulysses, 0)
    lax.fori_loop(0, 28, hail_plane, 0)
    w_local = pltpu.make_async_copy(
        w_in.at[:, pl.ds(pl.multiple_of(s * COLS, 128), COLS)],
        wf.at[pl.ds(pl.multiple_of(z * HD, 128), HD)],
        w_l,
    )
    w_local.start()
    pl.semaphore_wait(barrier, 59)

    mine = pl.ds(pl.multiple_of(u * OWN, 16), OWN)
    for i, (src, dst) in enumerate(((k_in, kb.at[x]), (v_in, vb.at[x]), (q_in, qb.at[k]))):

        def send_head(d, c, src=src, dst=dst, i=i):
            t = (u + d) % 32
            remote(
                src.at[:, pl.ds(pl.multiple_of(t * HD, 128), HD)], dst.at[mine], a2a_s.at[i], a2a_r.at[i], (s, t)
            ).start()
            return c

        lax.fori_loop(1, 32, send_head, 0)
        pltpu.make_async_copy(
            src.at[:, pl.ds(pl.multiple_of(u * HD, 128), HD)], dst.at[mine], a2a_r.at[i]
        ).start()

    level = levels[s]
    pick = (lax.broadcasted_iota(jnp.int32, (8, 64), 1) == level).astype(bf16)

    def to_chip(buf, slot, send_sem, recv_sem, chip):
        return remote(buf.at[slot], buf.at[slot], send_sem, recv_sem.at[slot], (chip * 2 + k, u))

    k_sends = {
        (0, 1): to_chip(kb, 0, kx_s.at[0], kx_r, 1),
        (0, 3): to_chip(kb, 0, kx_s.at[1], kx_r, 3),
        (1, 2): to_chip(kb, 1, kx_s.at[0], kx_r, 2),
        (1, 0): to_chip(kb, 1, kx_s.at[1], kx_r, 0),
        (2, 3): to_chip(kb, 2, kx_s.at[0], kx_r, 3),
    }
    k_relays = {
        (0, 3): to_chip(kb, 1, kx_s.at[2], kx_r, 3),
        (3, 2): to_chip(kb, 0, kx_s.at[2], kx_r, 2),
    }
    v_sends = {
        (0, 1): to_chip(vb, 0, vx_s.at[0], vx_r, 1),
        (0, 3): to_chip(vb, 0, vx_s.at[1], vx_r, 3),
        (1, 2): to_chip(vb, 1, vx_s.at[0], vx_r, 2),
        (2, 3): to_chip(vb, 2, vx_s.at[0], vx_r, 3),
    }
    v_relays = {
        (2, 3): to_chip(vb, 1, vx_s.at[2], vx_r, 3),
        (3, 2): to_chip(vb, 0, vx_s.at[2], vx_r, 2),
    }

    def start_all(copies):
        for (at, _), copy in copies.items():
            pl.when(x == at)(copy.start)

    def arrived(buf, sem, slot):
        wait_bytes(buf.at[slot], sem.at[slot])

    wait_bytes(kb.at[x], a2a_r.at[0])
    start_all(k_sends)
    pl.when(x == 0)(lambda: arrived(kb, kx_r, 1))
    pl.when(x == 3)(lambda: arrived(kb, kx_r, 0))
    start_all(k_relays)
    wait_bytes(vb.at[x], a2a_r.at[1])
    start_all(v_sends)
    pl.when(x == 2)(lambda: arrived(vb, vx_r, 1))
    pl.when(x == 3)(lambda: arrived(vb, vx_r, 0))
    start_all(v_relays)

    wait_bytes(qb.at[k], a2a_r.at[2])
    q_send = remote(qb.at[k], qb.at[k], qx_s, qx_r, (sib, u))
    q_send.start()

    w_local.wait()
    w_mine = pl.ds(pl.multiple_of(z * HD, 128), HD)

    def send_w(d, c):
        t = (z + d) % Z
        remote(wf.at[w_mine], wf.at[w_mine], w_s, w_r, (s, t * Y + y)).start()
        return c

    lax.fori_loop(1, Z, send_w, 0)

    pl.when(x == 1)(lambda: arrived(kb, kx_r, 0))
    pl.when(x == 1)(lambda: arrived(vb, vx_r, 0))
    for slot in (0, 1):
        pl.when(x == 2)(functools.partial(arrived, kb, kx_r, slot))
    pl.when(x == 2)(lambda: arrived(vb, vx_r, 0))
    for slot in (1, 2):
        pl.when(x == 3)(functools.partial(arrived, kb, kx_r, slot))
        pl.when(x == 3)(functools.partial(arrived, vb, vx_r, slot))

    def turn(i, c):
        vt[i] = vb[i].T
        return c

    lax.fori_loop(0, x + 1, turn, 0)

    def attend(which, span, half, low, count):
        q = qb[which, pl.ds(pl.multiple_of(half * HALF, 16), HALF)]
        start = first[span]

        def scores(chip, j):
            return lax.dot_general(
                kb[chip, pl.ds(j * KC, KC)], q, (((1,), (1,)), ((), ())), preferred_element_type=f32
            )

        def absorb(i, state):
            chip = low + count - 1 - i
            seen = 2 * chip + k >= start
            now = scores(chip, 0)
            for j in range(TOK // KC):
                later = scores(chip, j + 1) if j + 1 < TOK // KC else None
                top, total, accum = state
                new_top = jnp.maximum(top, jnp.where(seen, jnp.max(now, axis=0, keepdims=True), LOW))
                expo = jnp.exp2(now * C - jnp.where(seen, new_top * C, -LOW))
                shrink = jnp.exp2((top - new_top) * C)
                total = total * shrink + jnp.sum(expo, axis=0, keepdims=True)
                summed = jnp.dot(vt[chip, :, pl.ds(j * KC, KC)], expo.astype(bf16), preferred_element_type=f32)
                state = (new_top, total, accum * shrink + summed)
                now = later
            return state

        begin = (jnp.full((1, HALF), LOW, f32), jnp.zeros((1, HALF), f32), jnp.zeros((HD, HALF), f32))
        return lax.fori_loop(0, count, absorb, begin)

    wait_bytes(qb.at[1 - k], qx_r)

    last = x == 3
    sib_low = jnp.where(last & (k == 0), 2, 0)
    sib_count = x + 1 - k - sib_low
    own_low = jnp.where(last & (k == 1), 1, 0)
    own_count = x + 1 - own_low

    def give(half, c):
        top, total, accum = attend(1 - k, sib, half, sib_low, sib_count)
        po_s[half, pl.ds(0, HD)] = accum
        po_s[half, pl.ds(HD, 1)] = top
        po_s[half, pl.ds(HD + 1, 1)] = total
        remote(po_s.at[half], po_r.at[half], po_ss.at[half], po_rs.at[half], (sib, u)).start()
        return c

    lax.fori_loop(0, 2, give, 0)

    head_cols = pl.ds(pl.multiple_of(z * HD, 128), HD)

    def finish(half, c):
        top, total, accum = attend(k, s, half, own_low, own_count)
        wait_bytes(po_r.at[half], po_rs.at[half])
        top2 = po_r[half, pl.ds(HD, 1)]
        total2 = po_r[half, pl.ds(HD + 1, 1)]
        both = jnp.maximum(top, top2)
        one = jnp.exp2((top - both) * C)
        two = jnp.exp2((top2 - both) * C)
        inv = 1.0 / (total * one + total2 * two)
        attn = accum * (one * inv) + po_r[half, pl.ds(0, HD)] * (two * inv)
        ob[pl.ds(pl.multiple_of(half * HALF, 16), HALF)] = attn.T.astype(bf16)

        def send_slab(i, c):
            t = half * (Z // 2) + i
            rows = ob.at[pl.ds(pl.multiple_of(t * SLAB, 16), SLAB)]
            there = ag.at[s, :, head_cols]

            @pl.when(t != z)
            def _():
                remote(rows, there, oz_s, oz_r, (s, t * Y + y)).start()

            @pl.when(t == z)
            def _():
                pltpu.make_async_copy(rows, there, oz_r).start()

            return c

        lax.fori_loop(0, Z // 2, send_slab, 0)
        return c

    lax.fori_loop(0, 2, finish, 0)
    wait_bytes(ag.at[s], oz_r)

    def ag_copy(slot, i, to):
        return remote(ag.at[slot], ag.at[slot], ag_s.at[i], ag_r.at[slot], (to, u))

    ag_sends = [ag_copy(s, d - 1, ((x + d) % X) * 2 + k) for d in range(1, X)] + [ag_copy(s, 3, sib)]
    for copy in (ag_sends[0], ag_sends[2], ag_sends[1], ag_sends[3]):
        copy.start()

    wait_bytes(wf.at[pl.ds(0, 7 * HD)], w_r)

    def project(span):
        part = jnp.dot(ag[span], wf[...], preferred_element_type=f32).astype(bf16)
        pb[pl.ds(pl.multiple_of(span * SLAB, 16), SLAB)] = part
        there = rb.at[y, :, pl.ds(pl.multiple_of(s * COLS, 128), COLS)]

        def send_block(t, c):
            rows = pb.at[pl.ds(pl.multiple_of(span * SLAB + t * OWN, 16), OWN)]
            here = (span == s) & (t == y)

            @pl.when(here)
            def _():
                pltpu.make_async_copy(rows, there, y_r).start()

            @pl.when(jnp.logical_not(here))
            def _():
                remote(rows, there, y_s, y_r, (span, z * Y + t)).start()

            return c

        lax.fori_loop(0, Y, send_block, 0)

    project(s)
    wait_bytes(ag.at[sib], ag_r.at[sib])
    project(sib)
    relays = []
    for i, d in enumerate((1, 3, 2)):
        same = ((x + d) % X) * 2 + k
        wait_bytes(ag.at[same], ag_r.at[same])
        relay = ag_copy(same, 4 + i, sib)
        relay.start()
        relays.append(relay)
        project(same)
        other = ((x + d) % X) * 2 + 1 - k
        wait_bytes(ag.at[other], ag_r.at[other])
        project(other)

    gate = jnp.dot(pick, gate_in[...], preferred_element_type=f32)[0:1]
    wait_bytes(rb, y_r)
    total = rb[0].astype(f32)
    for i in range(1, Y):
        total = total + rb[i].astype(f32)
    out[...] = (gate * total).astype(bf16)

    for i, buf in enumerate((kb.at[x], vb.at[x], qb.at[k])):
        wait_bytes(buf.at[pl.ds(0, 31 * OWN)], a2a_s.at[i])
    for copies in (k_sends, k_relays, v_sends, v_relays):
        for (at, _), copy in copies.items():
            pl.when(x == at)(copy.wait_send)
    q_send.wait_send()
    for half in range(2):
        wait_bytes(po_s.at[half], po_ss.at[half])
    wait_bytes(ob.at[pl.ds(0, 7 * SLAB)], oz_s)
    wait_bytes(wf.at[pl.ds(0, 7 * HD)], w_s)
    for copy in ag_sends + relays:
        copy.wait_send()
    wait_bytes(pb.at[pl.ds(0, 31 * OWN)], y_s)


def shards(query, keys_in, values_in, out_weight, gate_table, levels, first_visible):
    vmem = pl.BlockSpec(memory_space=pltpu.VMEM)
    smem = pl.BlockSpec(memory_space=pltpu.SMEM)
    dma = pltpu.SemaphoreType.DMA
    out = pl.pallas_call(
        kernel,
        out_shape=jax.ShapeDtypeStruct((OWN, WIDE), bf16),
        in_specs=[vmem, vmem, vmem, pl.BlockSpec(memory_space=pl.ANY), vmem, smem, smem],
        out_specs=vmem,
        scratch_shapes=[
            pltpu.VMEM((2, TOK, HD), bf16),
            pltpu.VMEM((X, TOK, HD), bf16),
            pltpu.VMEM((X, TOK, HD), bf16),
            pltpu.VMEM((X, HD, TOK), bf16),
            pltpu.VMEM((2, HD + 8, HALF), f32),
            pltpu.VMEM((2, HD + 8, HALF), f32),
            pltpu.VMEM((TOK, HD), bf16),
            pltpu.VMEM((8, SLAB, Z * HD), bf16),
            pltpu.VMEM((Z * HD, COLS), bf16),
            pltpu.VMEM((8 * SLAB, COLS), bf16),
            pltpu.VMEM((Y, OWN, WIDE), bf16),
            dma((3,)), dma((3,)),
            dma((3,)), dma((X,)), dma((3,)), dma((X,)),
            dma, dma,
            dma((2,)), dma((2,)),
            dma, dma,
            dma((7,)), dma((8,)),
            dma, dma, dma,
            dma, dma,
        ],
        compiler_params=pltpu.CompilerParams(
            collective_id=0, has_side_effects=True, vmem_limit_bytes=56 * 2**20
        ),
    )(query[0], keys_in[0], values_in[0], out_weight, gate_table, levels, first_visible)
    return out[None]


def solution(mesh):
    placed = (
        P("span", "ulysses", None),
        P("span", "ulysses", None),
        P("span", "ulysses", None),
        P("ulysses", None),
        P(),
        P(),
        P(),
    )
    return jax.shard_map(
        shards, mesh=mesh, in_specs=placed, out_specs=P("span", "ulysses", None), check_vma=False
    )
```

```python
import functools
import math

import jax
import jax.numpy as jnp
from jax import lax
from jax.experimental import pallas as pl
from jax.experimental.pallas import tpu as pltpu
from jax.sharding import PartitionSpec as P

MESH = pl.DeviceIdType.MESH
f32, bf16 = jnp.float32, jnp.bfloat16

HD = 128
TOK = 1536
OWN = 48
Z, Y, X = 8, 4, 4
WIDE = 6144
COLS = WIDE // 8
PASS = 3
PTOK = TOK // PASS
POWN = OWN // PASS
SLAB = Y * POWN
KC = 512
C = math.log2(math.e) / math.sqrt(HD)
LOW = -1e30


def remote(src, dst, send_sem, recv_sem, device):
    return pltpu.make_async_remote_copy(
        src_ref=src, dst_ref=dst, send_sem=send_sem, recv_sem=recv_sem, device_id=device, device_id_type=MESH
    )


def wait_bytes(ref, sem):
    pltpu.make_async_copy(ref, ref, sem).wait()


def aligned(index, size, multiple):
    return pl.ds(pl.multiple_of(index * size, multiple), size)


def kernel(
    q_in, k_in, v_in, w_in, gate_in, levels, first, out,
    qb, kb, vb, vt, st, po_r, ob, ag, wf, gt, gs, pb, yb, xb,
    a2a_s, a2a_r, kx_s, kx_r, vx_s, vx_r, qx_s, qx_r, po_ss, po_rs, oz_s, oz_r, ag_s, ag_r,
    wl, wp_s, wp_r, wm_s, wm_r, y_s, y_r, x_s, x_r,
):
    s, u = lax.axis_index("span"), lax.axis_index("ulysses")
    x, k = s // 2, s % 2
    z, y = u // Y, u % Y
    sib = x * 2 + (1 - k)
    my_cols = aligned(s, COLS, 128)

    barrier = pltpu.get_barrier_semaphore()

    def hail_ulysses(d, c):
        pl.semaphore_signal(barrier, inc=1, device_id=(s, (u + d) % 32), device_id_type=MESH)
        return c

    def hail_span(d, c):
        pl.semaphore_signal(barrier, inc=1, device_id=((s + d) % 8, u), device_id_type=MESH)
        return c

    lax.fori_loop(1, 32, hail_ulysses, 0)
    lax.fori_loop(1, 8, hail_span, 0)
    w_local = pltpu.make_async_copy(w_in.at[:, my_cols], wf.at[aligned(z, HD, 128)], wl.at[0])
    w_local.start()
    g_local = pltpu.make_async_copy(gate_in.at[:, my_cols], gt, wl.at[1])
    g_local.start()
    pl.semaphore_wait(barrier, 38)

    mine = aligned(u, OWN, 16)
    mine_q = aligned(u, POWN, 16)
    moves = (
        (lambda t: k_in.at[:, aligned(t, HD, 128)], kb.at[x, mine]),
        (lambda t: v_in.at[:, aligned(t, HD, 128)], vb.at[x, mine]),
        (lambda t: q_in.at[:, :, aligned(t, HD, 128)], qb.at[:, k, mine_q]),
    )
    for i, (src, dst) in enumerate(moves):

        def send_head(d, c, src=src, dst=dst, i=i):
            t = (u + d) % 32
            remote(src(t), dst, a2a_s.at[i], a2a_r.at[i], (s, t)).start()
            return c

        lax.fori_loop(1, 32, send_head, 0)
        pltpu.make_async_copy(src(u), dst, a2a_r.at[i]).start()

    pick = jnp.zeros((8, 64), f32)
    rows8 = lax.broadcasted_iota(jnp.int32, (8, 64), 0)
    cols64 = lax.broadcasted_iota(jnp.int32, (8, 64), 1)
    for c in range(8):
        pick = jnp.where((rows8 == c) & (cols64 == levels[c]), 1.0, pick)
    g_local.wait()
    gs[...] = jnp.dot(pick.astype(bf16), gt[...], preferred_element_type=f32)

    st[:, :, 0:HD] = jnp.zeros((PASS, 2, HD, PTOK), f32)
    st[:, :, HD : HD + 1] = jnp.full((PASS, 2, 1, PTOK), LOW, f32)
    st[:, :, HD + 1 : HD + 2] = jnp.zeros((PASS, 2, 1, PTOK), f32)

    def along(buf, sends, recvs, slot, i, chip, j):
        part = buf.at[slot, pl.ds(j * KC, KC)]
        return remote(part, part, sends.at[i, j], recvs.at[slot, j], (chip * 2 + k, u))

    k_sends = ((0, 0, 0, 1), (0, 0, 1, 3), (1, 1, 0, 2), (1, 1, 1, 0), (2, 2, 0, 3))
    k_relays = ((0, 1, 2, 3), (3, 0, 2, 2))
    v_sends = ((0, 0, 0, 1), (0, 0, 1, 3), (1, 1, 0, 2), (2, 2, 0, 3))
    v_relays = ((2, 1, 2, 3), (1, 0, 2, 2))
    chunks = TOK // KC
    drains = []

    def start_chunk(buf, sends, recvs, entry, j):
        at, slot, i, chip = entry
        copy = along(buf, sends, recvs, slot, i, chip, j)
        pl.when(x == at)(copy.start)
        drains.append(lambda: pl.when(x == at)(copy.wait_send))

    def arrived(buf, recvs, slot, j):
        wait_bytes(buf.at[slot, pl.ds(j * KC, KC)], recvs.at[slot, j])

    def exchange(buf, sends, recvs, direct, relays):
        for j in range(chunks):
            for entry in direct:
                start_chunk(buf, sends, recvs, entry, j)
        for j in range(chunks):
            for entry in relays:
                pl.when(x == entry[0])(functools.partial(arrived, buf, recvs, entry[1], j))
                start_chunk(buf, sends, recvs, entry, j)

    def await_rest(wanted):
        for at, buf, recvs, slot in wanted:

            @pl.when(x == at)
            def _():
                for j in range(chunks):
                    arrived(buf, recvs, slot, j)

    def turn(chip, c):
        vt[chip] = vb[chip].T
        return c

    wait_bytes(kb.at[x], a2a_r.at[0])
    exchange(kb, kx_s, kx_r, k_sends, k_relays)
    wait_bytes(vb.at[x], a2a_r.at[1])
    exchange(vb, vx_s, vx_r, v_sends, v_relays)
    turn(x, 0)

    wait_bytes(qb.at[:, k], a2a_r.at[2])
    q_send = remote(qb.at[:, k], qb.at[:, k], qx_s, qx_r, (sib, u))
    q_send.start()

    def w_copies(t):
        up, down = (z + Z - t + 1) % Z, (z + t - 1) % Z
        size, shift = (HD, 0) if t < Z // 2 else (HD // 2, HD // 2)
        one = wf.at[pl.ds(pl.multiple_of(up * HD, 64), size)]
        two = wf.at[pl.ds(pl.multiple_of(down * HD + shift, 64), size)]
        i = t - 1
        return (
            remote(one, one, wp_s.at[i], wp_r.at[i], (s, (z + 1) % Z * Y + y)),
            remote(two, two, wm_s.at[i], wm_r.at[i], (s, (z + Z - 1) % Z * Y + y)),
        )

    def w_step(t):
        if t == 1:
            w_local.wait()
        else:
            for copy in w_copies(t - 1):
                copy.wait_recv()
        if t <= Z // 2:
            for copy in w_copies(t):
                copy.start()
                drains.append(copy.wait_send)

    w_step(1)

    even, odd = first[x * 2], first[x * 2 + 1]

    def absorb(q, chip, seen, state):
        def scores(j):
            return lax.dot_general(
                kb[chip, pl.ds(j * KC, KC)], q, (((1,), (1,)), ((), ())), preferred_element_type=f32
            )

        now = scores(0)
        for j in range(chunks):
            later = scores(j + 1) if j + 1 < chunks else None
            top, total, accum = state
            new_top = jnp.maximum(top, jnp.where(seen, jnp.max(now, axis=0, keepdims=True), LOW))
            expo = jnp.exp2(now * C - jnp.where(seen, new_top * C, -LOW))
            shrink = jnp.exp2((top - new_top) * C)
            total = total * shrink + jnp.sum(expo, axis=0, keepdims=True)
            summed = jnp.dot(vt[chip, :, pl.ds(j * KC, KC)], expo.astype(bf16), preferred_element_type=f32)
            state = (new_top, total, accum * shrink + summed)
            now = later
        return state

    def load(p, w):
        return st[p, w, pl.ds(HD, 1)], st[p, w, pl.ds(HD + 1, 1)], st[p, w, pl.ds(0, HD)]

    def store(p, w, state):
        top, total, accum = state
        st[p, w, pl.ds(0, HD)] = accum
        st[p, w, pl.ds(HD, 1)] = top
        st[p, w, pl.ds(HD + 1, 1)] = total

    def pair(p, low, high):
        @pl.when(high >= low)
        def _():
            q = qb[p].reshape(2 * PTOK, HD)
            which = lax.broadcasted_iota(jnp.int32, (1, 2 * PTOK), 1) // PTOK
            start = jnp.where(which == 0, even, odd)

            def step(i, state):
                chip = high - i
                return absorb(q, chip, 2 * chip + k >= start, state)

            state = tuple(jnp.concatenate(pieces, axis=1) for pieces in zip(load(p, 0), load(p, 1)))
            state = lax.fori_loop(0, high - low + 1, step, state)
            for w in range(2):
                store(p, w, tuple(piece[:, w * PTOK : (w + 1) * PTOK] for piece in state))

    def single(p, w, start, low, high):
        @pl.when(high >= low)
        def _():
            q = qb[p, w]

            def step(i, state):
                chip = high - i
                return absorb(q, chip, 2 * chip + k >= start, state)

            store(p, w, lax.fori_loop(0, high - low + 1, step, load(p, w)))

    share = [remote(st.at[p, 1 - k], po_r.at[p], po_ss.at[p], po_rs.at[p], (sib, u)) for p in range(PASS)]

    def near(p):
        single(p, 1, odd, x, jnp.where(k == 1, x, x - 1))
        pair(p, jnp.maximum(x - 1, 0), x - k)

    def far(p):
        chip = jnp.where(x == 3, 1, 0)
        pair(p, chip, jnp.where((x == 2) | ((x == 3) & (k == 1)), chip, -1))
        pl.when(k == 0)(share[p].start)
        single(p, 0, even, 0, jnp.where(x == 3, 1 - k, -1))
        pl.when(k == 1)(share[p].start)
        drains.append(share[p].wait_send)

    def finish(p):
        wait_bytes(po_r.at[p], po_rs.at[p])
        top, total, accum = load(p, k)
        top2, total2 = po_r[p, HD : HD + 1], po_r[p, HD + 1 : HD + 2]
        both = jnp.maximum(top, top2)
        one_s = jnp.exp2((top - both) * C)
        two_s = jnp.exp2((top2 - both) * C)
        inv = 1.0 / (total * one_s + total2 * two_s)
        attn = accum * (one_s * inv) + po_r[p, 0:HD] * (two_s * inv)
        ob[p] = attn.astype(bf16).T
        there = ag.at[p, s, :, aligned(z, HD, 128)]

        def send_slab(d, c):
            t = (z + d) % Z
            remote(ob.at[p, aligned(t, SLAB, 16)], there, oz_s.at[p], oz_r.at[p], (s, t * Y + y)).start()
            return c

        lax.fori_loop(1, Z, send_slab, 0)
        pltpu.make_async_copy(ob.at[p, aligned(z, SLAB, 16)], there, oz_r.at[p]).start()
        drains.append(lambda: wait_bytes(ob.at[p, pl.ds(0, (Z - 1) * SLAB)], oz_s.at[p]))

    def ag_copy(p, slot, i, to):
        return remote(ag.at[p, slot], ag.at[p, slot], ag_s.at[p, i], ag_r.at[p, slot], (to, u))

    def gather(p):
        wait_bytes(ag.at[p, s], oz_r.at[p])
        for i, to in enumerate([((x + d) % X) * 2 + k for d in (1, 3, 2)] + [sib]):
            copy = ag_copy(p, s, i, to)
            copy.start()
            drains.append(copy.wait_send)

    def pass_on(p):
        for i, d in enumerate((1, 3, 2)):
            slot = ((x + d) % X) * 2 + k
            wait_bytes(ag.at[p, slot], ag_r.at[p, slot])
            copy = ag_copy(p, slot, 4 + i, sib)
            copy.start()
            drains.append(copy.wait_send)

    def project(p):
        for d in range(X):
            slot = ((x + d) % X) * 2 + 1 - k
            wait_bytes(ag.at[p, slot], ag_r.at[p, slot])
        part = jnp.dot(ag[p].reshape(8 * SLAB, Z * HD), wf[...], preferred_element_type=f32)
        pb[p] = part.astype(bf16).reshape(8, Y, POWN, COLS)
        for i, d in enumerate((1, 3, 2)):
            t = (y + d) % Y
            copy = remote(pb.at[p, :, t], yb.at[p, y], y_s.at[p, i], y_r.at[p, y], (s, z * Y + t))
            copy.start()
            drains.append(copy.wait_send)

    def settle(p):
        total = pb[p, :, y].astype(f32)
        for d in (1, 3, 2):
            t = (y + d) % Y
            wait_bytes(yb.at[p, t], y_r.at[p, t])
            total = total + yb[p, t].astype(f32)
        xb[p] = (total * gs[...].reshape(8, 1, COLS)).astype(bf16)
        there = out.at[pl.ds(p * POWN, POWN), my_cols]
        for i in range(1, 8):
            t = (s + i) % 8
            copy = remote(xb.at[p, t], there, x_s.at[p, i - 1], x_r.at[p], (t, u))
            copy.start()
            drains.append(copy.wait_send)
        pltpu.make_async_copy(xb.at[p, s], there, x_r.at[p]).start()

    await_rest(((1, kb, kx_r, 0), (2, kb, kx_r, 1), (3, kb, kx_r, 2), (3, vb, vx_r, 2)))
    lax.fori_loop(jnp.maximum(x - 1, 0), x, turn, 0)
    wait_bytes(qb.at[:, 1 - k], qx_r)

    def late():
        await_rest(
            ((2, kb, kx_r, 0), (2, vb, vx_r, 0), (3, vb, vx_r, 0), (3, kb, kx_r, 1), (3, vb, vx_r, 1))
        )
        lax.fori_loop(0, jnp.maximum(x - 1, 0), turn, 0)

    near(0)
    w_step(2)
    near(1)
    late()
    far(0)
    w_step(3)
    far(1)
    finish(0)
    near(2)
    w_step(4)
    finish(1)
    gather(0)
    far(2)
    gather(1)
    w_step(5)
    finish(2)
    pass_on(0)
    project(0)
    pass_on(1)
    project(1)
    gather(2)
    settle(0)
    pass_on(2)
    project(2)
    settle(1)
    settle(2)
    for p in range(PASS):
        rows = out.at[pl.ds(p * POWN, POWN)]
        wait_bytes(rows, x_r.at[p])

    for i, buf in enumerate((kb.at[x], vb.at[x])):
        wait_bytes(buf.at[pl.ds(0, 31 * OWN)], a2a_s.at[i])
    wait_bytes(kb.at[x].at[pl.ds(0, 31 * OWN)], a2a_s.at[2])
    q_send.wait_send()
    for drain in drains:
        drain()


def shards(query, keys_in, values_in, out_weight, gate_table, levels, first_visible):
    anywhere = pl.BlockSpec(memory_space=pl.ANY)
    smem = pl.BlockSpec(memory_space=pltpu.SMEM)
    dma = pltpu.SemaphoreType.DMA
    vmem = pltpu.VMEM
    out = pl.pallas_call(
        kernel,
        out_shape=jax.ShapeDtypeStruct((OWN, WIDE), bf16),
        in_specs=[anywhere] * 5 + [smem, smem],
        out_specs=pl.BlockSpec(memory_space=pltpu.VMEM),
        scratch_shapes=[
            vmem((PASS, 2, PTOK, HD), bf16),
            vmem((X, TOK, HD), bf16),
            vmem((X, TOK, HD), bf16),
            vmem((X, HD, TOK), bf16),
            vmem((PASS, 2, HD + 8, PTOK), f32),
            vmem((PASS, HD + 8, PTOK), f32),
            vmem((PASS, PTOK, HD), bf16),
            vmem((PASS, 8, SLAB, Z * HD), bf16),
            vmem((Z * HD, COLS), bf16),
            vmem((64, COLS), bf16),
            vmem((8, COLS), f32),
            vmem((PASS, 8, Y, POWN, COLS), bf16),
            vmem((PASS, Y, 8, POWN, COLS), bf16),
            vmem((PASS, 8, POWN, COLS), bf16),
            dma((3,)), dma((3,)),
            dma((3, 3)), dma((X, 3)), dma((3, 3)), dma((X, 3)),
            dma, dma,
            dma((PASS,)), dma((PASS,)),
            dma((PASS,)), dma((PASS,)),
            dma((PASS, 7)), dma((PASS, 8)),
            dma((2,)), dma((4,)), dma((4,)), dma((4,)), dma((4,)),
            dma((PASS, 3)), dma((PASS, Y)),
            dma((PASS, 7)), dma((PASS,)),
        ],
        compiler_params=pltpu.CompilerParams(
            collective_id=0, has_side_effects=True, vmem_limit_bytes=56 * 2**20
        ),
    )(
        query.reshape(PASS, POWN, query.shape[2]), keys_in[0], values_in[0], out_weight, gate_table, levels,
        first_visible,
    )
    return out[None]


def solution(mesh):
    placed = (
        P("span", "ulysses", None),
        P("span", "ulysses", None),
        P("span", "ulysses", None),
        P("ulysses", None),
        P(),
        P(),
        P(),
    )
    return jax.shard_map(
        shards, mesh=mesh, in_specs=placed, out_specs=P("span", "ulysses", None), check_vma=False
    )
```

```python
import functools
import math

import jax
import jax.numpy as jnp
from jax import lax
from jax.experimental import pallas as pl
from jax.experimental.pallas import tpu as pltpu
from jax.sharding import PartitionSpec as P

MESH = pl.DeviceIdType.MESH
f32, bf16 = jnp.float32, jnp.bfloat16

HD = 128
TOK = 1536
OWN = 48
Z, Y, X = 8, 4, 4
WIDE = 6144
COLS = WIDE // 8
PASS = 3
PTOK = TOK // PASS
POWN = OWN // PASS
SLAB = Y * POWN
KC = 512
C = math.log2(math.e) / math.sqrt(HD)
LOW = -1e30
FIRST, LAST = slice(0, 4), slice(4, 8)


def remote(src, dst, send_sem, recv_sem, device):
    return pltpu.make_async_remote_copy(
        src_ref=src, dst_ref=dst, send_sem=send_sem, recv_sem=recv_sem, device_id=device, device_id_type=MESH
    )


def wait_bytes(ref, sem):
    pltpu.make_async_copy(ref, ref, sem).wait()


def aligned(index, size, multiple):
    return pl.ds(pl.multiple_of(index * size, multiple), size)


def kernel(
    q_in, k_in, v_in, w_in, gate_in, levels, first, out,
    qb, kb, vb, vt, st, po_r, ob, ag, wf, gt, gs, pb, hb, cb, yb, xb,
    a2a_s, a2a_r, kx_s, kx_r, vx_s, vx_r, qx_s, qx_r, po_ss, po_rs, oz_s, oz_r, ag_s, ag_r,
    wl, wp_s, wp_r, wm_s, wm_r, y_s, y_r, x_s, x_r,
):
    s, u = lax.axis_index("span"), lax.axis_index("ulysses")
    x, k = s // 2, s % 2
    z, y = u // Y, u % Y
    sib = x * 2 + (1 - k)
    my_cols = aligned(s, COLS, 128)

    barrier = pltpu.get_barrier_semaphore()

    def hail_ulysses(d, c):
        pl.semaphore_signal(barrier, inc=1, device_id=(s, (u + d) % 32), device_id_type=MESH)
        return c

    def hail_span(d, c):
        pl.semaphore_signal(barrier, inc=1, device_id=((s + d) % 8, u), device_id_type=MESH)
        return c

    lax.fori_loop(1, 32, hail_ulysses, 0)
    lax.fori_loop(1, 8, hail_span, 0)
    w_local = pltpu.make_async_copy(w_in.at[:, my_cols], wf.at[aligned(z, HD, 128)], wl.at[0])
    w_local.start()
    g_local = pltpu.make_async_copy(gate_in.at[:, my_cols], gt, wl.at[1])
    g_local.start()
    pl.semaphore_wait(barrier, 38)

    mine = aligned(u, OWN, 16)
    mine_q = aligned(u, POWN, 16)
    moves = (
        (lambda t: k_in.at[:, aligned(t, HD, 128)], kb.at[x, mine]),
        (lambda t: v_in.at[:, aligned(t, HD, 128)], vb.at[x, mine]),
        (lambda t: q_in.at[:, :, aligned(t, HD, 128)], qb.at[:, k, mine_q]),
    )
    for i, (src, dst) in enumerate(moves):

        def send_head(d, c, src=src, dst=dst, i=i):
            t = (u + d) % 32
            remote(src(t), dst, a2a_s.at[i], a2a_r.at[i], (s, t)).start()
            return c

        lax.fori_loop(1, 32, send_head, 0)
        pltpu.make_async_copy(src(u), dst, a2a_r.at[i]).start()

    pick = jnp.zeros((8, 64), f32)
    rows8 = lax.broadcasted_iota(jnp.int32, (8, 64), 0)
    cols64 = lax.broadcasted_iota(jnp.int32, (8, 64), 1)
    for c in range(8):
        pick = jnp.where((rows8 == c) & (cols64 == levels[c]), 1.0, pick)
    g_local.wait()
    gs[...] = jnp.dot(pick.astype(bf16), gt[...], preferred_element_type=f32)

    st[:, :, 0:HD] = jnp.zeros((PASS, 2, HD, PTOK), f32)
    st[:, :, HD : HD + 1] = jnp.full((PASS, 2, 1, PTOK), LOW, f32)
    st[:, :, HD + 1 : HD + 2] = jnp.zeros((PASS, 2, 1, PTOK), f32)

    def along(buf, sends, recvs, slot, i, chip, j):
        part = buf.at[slot, pl.ds(j * KC, KC)]
        return remote(part, part, sends.at[i, j], recvs.at[slot, j], (chip * 2 + k, u))

    k_sends = ((0, 0, 0, 1), (0, 0, 1, 3), (1, 1, 0, 2), (1, 1, 1, 0), (2, 2, 0, 3))
    k_relays = ((0, 1, 2, 3), (3, 0, 2, 2))
    v_sends = ((0, 0, 0, 1), (0, 0, 1, 3), (1, 1, 0, 2), (2, 2, 0, 3))
    v_relays = ((2, 1, 2, 3), (1, 0, 2, 2))
    chunks = TOK // KC
    drains = []

    def start_chunk(buf, sends, recvs, entry, j):
        at, slot, i, chip = entry
        copy = along(buf, sends, recvs, slot, i, chip, j)
        pl.when(x == at)(copy.start)
        drains.append(lambda: pl.when(x == at)(copy.wait_send))

    def arrived(buf, recvs, slot, j):
        wait_bytes(buf.at[slot, pl.ds(j * KC, KC)], recvs.at[slot, j])

    def exchange(buf, sends, recvs, direct, relays):
        for j in range(chunks):
            for entry in direct:
                start_chunk(buf, sends, recvs, entry, j)
        for j in range(chunks):
            for entry in relays:
                pl.when(x == entry[0])(functools.partial(arrived, buf, recvs, entry[1], j))
                start_chunk(buf, sends, recvs, entry, j)

    def await_rest(wanted):
        for at, buf, recvs, slot in wanted:

            @pl.when(x == at)
            def _():
                for j in range(chunks):
                    arrived(buf, recvs, slot, j)

    def turn(chip, c):
        vt[chip] = vb[chip].T
        return c

    wait_bytes(kb.at[x], a2a_r.at[0])
    exchange(kb, kx_s, kx_r, k_sends, k_relays)
    wait_bytes(vb.at[x], a2a_r.at[1])
    exchange(vb, vx_s, vx_r, v_sends, v_relays)
    turn(x, 0)
    def w_copies(t):
        up, down = (z + Z - t + 1) % Z, (z + t - 1) % Z
        size, shift = (HD, 0) if t < Z // 2 else (HD // 2, HD // 2)
        one = wf.at[pl.ds(pl.multiple_of(up * HD, 64), size)]
        two = wf.at[pl.ds(pl.multiple_of(down * HD + shift, 64), size)]
        i = t - 1
        return (
            remote(one, one, wp_s.at[i], wp_r.at[i], (s, (z + 1) % Z * Y + y)),
            remote(two, two, wm_s.at[i], wm_r.at[i], (s, (z + Z - 1) % Z * Y + y)),
        )

    def w_step(t):
        if t == 1:
            w_local.wait()
        else:
            for copy in w_copies(t - 1):
                copy.wait_recv()
        if t <= Z // 2:
            for copy in w_copies(t):
                copy.start()
                drains.append(copy.wait_send)


    w_step(1)

    wait_bytes(qb.at[:, k], a2a_r.at[2])
    q_send = remote(qb.at[:, k], qb.at[:, k], qx_s, qx_r, (sib, u))
    q_send.start()

    even, odd = first[x * 2], first[x * 2 + 1]

    def absorb(q, chip, seen, state):
        def scores(j):
            return lax.dot_general(
                kb[chip, pl.ds(j * KC, KC)], q, (((1,), (1,)), ((), ())), preferred_element_type=f32
            )

        now = scores(0)
        for j in range(chunks):
            later = scores(j + 1) if j + 1 < chunks else None
            top, total, accum = state
            new_top = jnp.maximum(top, jnp.where(seen, jnp.max(now, axis=0, keepdims=True), LOW))
            expo = jnp.exp2(now * C - jnp.where(seen, new_top * C, -LOW))
            shrink = jnp.exp2((top - new_top) * C)
            total = total * shrink + jnp.sum(expo, axis=0, keepdims=True)
            summed = jnp.dot(vt[chip, :, pl.ds(j * KC, KC)], expo.astype(bf16), preferred_element_type=f32)
            state = (new_top, total, accum * shrink + summed)
            now = later
        return state

    def load(p, w):
        return st[p, w, pl.ds(HD, 1)], st[p, w, pl.ds(HD + 1, 1)], st[p, w, pl.ds(0, HD)]

    def store(p, w, state):
        top, total, accum = state
        st[p, w, pl.ds(0, HD)] = accum
        st[p, w, pl.ds(HD, 1)] = top
        st[p, w, pl.ds(HD + 1, 1)] = total

    def pair(p, low, high):
        @pl.when(high >= low)
        def _():
            q = qb[p].reshape(2 * PTOK, HD)
            which = lax.broadcasted_iota(jnp.int32, (1, 2 * PTOK), 1) // PTOK
            start = jnp.where(which == 0, even, odd)

            def step(i, state):
                chip = high - i
                return absorb(q, chip, 2 * chip + k >= start, state)

            state = tuple(jnp.concatenate(pieces, axis=1) for pieces in zip(load(p, 0), load(p, 1)))
            state = lax.fori_loop(0, high - low + 1, step, state)
            for w in range(2):
                store(p, w, tuple(piece[:, w * PTOK : (w + 1) * PTOK] for piece in state))

    def single(p, w, start, low, high):
        @pl.when(high >= low)
        def _():
            q = qb[p, w]

            def step(i, state):
                chip = high - i
                return absorb(q, chip, 2 * chip + k >= start, state)

            store(p, w, lax.fori_loop(0, high - low + 1, step, load(p, w)))

    share = [remote(st.at[p, 1 - k], po_r.at[p], po_ss.at[p], po_rs.at[p], (sib, u)) for p in range(PASS)]

    def near(p):
        single(p, 1, odd, x, jnp.where(k == 1, x, x - 1))
        pair(p, jnp.maximum(x - 1, 0), x - k)

    def far(p):
        chip = jnp.where(x == 3, 1, 0)
        pair(p, chip, jnp.where((x == 2) | ((x == 3) & (k == 1)), chip, -1))
        pl.when(k == 0)(share[p].start)
        single(p, 0, even, 0, jnp.where(x == 3, 1 - k, -1))
        pl.when(k == 1)(share[p].start)
        drains.append(share[p].wait_send)

    def finish(p):
        wait_bytes(po_r.at[p], po_rs.at[p])
        top, total, accum = load(p, k)
        top2, total2 = po_r[p, HD : HD + 1], po_r[p, HD + 1 : HD + 2]
        both = jnp.maximum(top, top2)
        one_s = jnp.exp2((top - both) * C)
        two_s = jnp.exp2((top2 - both) * C)
        inv = 1.0 / (total * one_s + total2 * two_s)
        attn = accum * (one_s * inv) + po_r[p, 0:HD] * (two_s * inv)
        ob[p] = attn.astype(bf16).T
        there = ag.at[p, s, :, aligned(z, HD, 128)]

        def send_slab(d, c):
            t = (z + d) % Z
            remote(ob.at[p, aligned(t, SLAB, 16)], there, oz_s.at[p], oz_r.at[p], (s, t * Y + y)).start()
            return c

        lax.fori_loop(1, Z, send_slab, 0)
        pltpu.make_async_copy(ob.at[p, aligned(z, SLAB, 16)], there, oz_r.at[p]).start()
        drains.append(lambda: wait_bytes(ob.at[p, pl.ds(0, (Z - 1) * SLAB)], oz_s.at[p]))

    above, below = (y + 1) % Y, (y + Y - 1) % Y

    def start(copy):
        copy.start()
        drains.append(copy.wait_send)

    def ag_copy(p, slot, i, to):
        return remote(ag.at[p, slot], ag.at[p, slot], ag_s.at[p, i], ag_r.at[p, slot], (to, u))

    def gather(p):
        wait_bytes(ag.at[p, s], oz_r.at[p])
        for i, to in enumerate([((x + d) % X) * 2 + k for d in (1, 3, 2)] + [sib]):
            copy = ag_copy(p, s, i, to)
            copy.start()
            drains.append(copy.wait_send)

    def pass_on(p):
        for i, d in enumerate((1, 3, 2)):
            slot = ((x + d) % X) * 2 + k
            wait_bytes(ag.at[p, slot], ag_r.at[p, slot])
            copy = ag_copy(p, slot, 4 + i, sib)
            copy.start()
            drains.append(copy.wait_send)

    def project(p):
        for d in range(X):
            slot = ((x + d) % X) * 2 + 1 - k
            wait_bytes(ag.at[p, slot], ag_r.at[p, slot])
        part = jnp.dot(ag[p].reshape(8 * SLAB, Z * HD), wf[...], preferred_element_type=f32)
        pb[p] = part.astype(bf16).reshape(8, Y, POWN, COLS)
        for w, (t, far_spans, near_spans) in enumerate(((above, FIRST, LAST), (below, LAST, FIRST))):
            opposite = (y + 2) % Y
            start(remote(pb.at[p, far_spans, opposite], hb.at[p, w], y_s.at[p, w, 0], y_r.at[p, w, 0], (s, z * Y + t)))
            start(remote(pb.at[p, near_spans, t], yb.at[p, w, 1], y_s.at[p, w, 1], y_r.at[p, w, 1], (s, z * Y + t)))

    def forward(p):
        for w, (t, far_spans) in enumerate(((above, FIRST), (below, LAST))):
            wait_bytes(hb.at[p, w], y_r.at[p, w, 0])
            both = hb[p, w].astype(f32) + pb[p, far_spans, t].astype(f32)
            cb[p, w] = both.astype(bf16)
            start(remote(cb.at[p, w], yb.at[p, w, 0], y_s.at[p, w, 2], y_r.at[p, w, 2], (s, z * Y + t)))

    def settle(p):
        for w in range(2):
            wait_bytes(yb.at[p, w, 1], y_r.at[p, w, 1])
            wait_bytes(yb.at[p, w, 0], y_r.at[p, w, 2])
        for w, spans in enumerate((FIRST, LAST)):
            total = pb[p, spans, y].astype(f32) + yb[p, w, 0].astype(f32) + yb[p, 1 - w, 1].astype(f32)
            xb[p, spans] = (total * gs[spans].reshape(4, 1, COLS)).astype(bf16)
        there = out.at[pl.ds(p * POWN, POWN), my_cols]
        for i in range(1, 8):
            t = (s + i) % 8
            copy = remote(xb.at[p, t], there, x_s.at[p, i - 1], x_r.at[p], (t, u))
            copy.start()
            drains.append(copy.wait_send)
        pltpu.make_async_copy(xb.at[p, s], there, x_r.at[p]).start()

    await_rest(((1, kb, kx_r, 0), (2, kb, kx_r, 1), (3, kb, kx_r, 2), (3, vb, vx_r, 2)))
    lax.fori_loop(jnp.maximum(x - 1, 0), x, turn, 0)
    wait_bytes(qb.at[:, 1 - k], qx_r)

    def late():
        await_rest(
            ((2, kb, kx_r, 0), (2, vb, vx_r, 0), (3, vb, vx_r, 0), (3, kb, kx_r, 1), (3, vb, vx_r, 1))
        )
        lax.fori_loop(0, jnp.maximum(x - 1, 0), turn, 0)

    near(0)
    w_step(2)
    near(1)
    late()
    far(0)
    w_step(3)
    far(1)
    finish(0)
    near(2)
    w_step(4)
    finish(1)
    gather(0)
    far(2)
    gather(1)
    w_step(5)
    finish(2)
    pass_on(0)
    project(0)
    gather(2)
    pass_on(1)
    forward(0)
    project(1)
    pass_on(2)
    forward(1)
    project(2)
    settle(0)
    settle(1)
    forward(2)
    settle(2)
    for p in range(PASS):
        rows = out.at[pl.ds(p * POWN, POWN)]
        wait_bytes(rows, x_r.at[p])

    for i, buf in enumerate((kb.at[x], vb.at[x])):
        wait_bytes(buf.at[pl.ds(0, 31 * OWN)], a2a_s.at[i])
    wait_bytes(kb.at[x].at[pl.ds(0, 31 * OWN)], a2a_s.at[2])
    q_send.wait_send()
    for drain in drains:
        drain()


def shards(query, keys_in, values_in, out_weight, gate_table, levels, first_visible):
    anywhere = pl.BlockSpec(memory_space=pl.ANY)
    smem = pl.BlockSpec(memory_space=pltpu.SMEM)
    dma = pltpu.SemaphoreType.DMA
    vmem = pltpu.VMEM
    out = pl.pallas_call(
        kernel,
        out_shape=jax.ShapeDtypeStruct((OWN, WIDE), bf16),
        in_specs=[anywhere] * 5 + [smem, smem],
        out_specs=pl.BlockSpec(memory_space=pltpu.VMEM),
        scratch_shapes=[
            vmem((PASS, 2, PTOK, HD), bf16),
            vmem((X, TOK, HD), bf16),
            vmem((X, TOK, HD), bf16),
            vmem((X, HD, TOK), bf16),
            vmem((PASS, 2, HD + 8, PTOK), f32),
            vmem((PASS, HD + 8, PTOK), f32),
            vmem((PASS, PTOK, HD), bf16),
            vmem((PASS, 8, SLAB, Z * HD), bf16),
            vmem((Z * HD, COLS), bf16),
            vmem((64, COLS), bf16),
            vmem((8, COLS), f32),
            vmem((PASS, 8, Y, POWN, COLS), bf16),
            vmem((PASS, 2, 4, POWN, COLS), bf16),
            vmem((PASS, 2, 4, POWN, COLS), bf16),
            vmem((PASS, 2, 2, 4, POWN, COLS), bf16),
            vmem((PASS, 8, POWN, COLS), bf16),
            dma((3,)), dma((3,)),
            dma((3, 3)), dma((X, 3)), dma((3, 3)), dma((X, 3)),
            dma, dma,
            dma((PASS,)), dma((PASS,)),
            dma((PASS,)), dma((PASS,)),
            dma((PASS, 7)), dma((PASS, 8)),
            dma((2,)), dma((4,)), dma((4,)), dma((4,)), dma((4,)),
            dma((PASS, 2, 3)), dma((PASS, 2, 3)),
            dma((PASS, 7)), dma((PASS,)),
        ],
        compiler_params=pltpu.CompilerParams(
            collective_id=0, has_side_effects=True, vmem_limit_bytes=56 * 2**20
        ),
    )(
        query.reshape(PASS, POWN, query.shape[2]), keys_in[0], values_in[0], out_weight, gate_table, levels,
        first_visible,
    )
    return out[None]


def solution(mesh):
    placed = (
        P("span", "ulysses", None),
        P("span", "ulysses", None),
        P("span", "ulysses", None),
        P("ulysses", None),
        P(),
        P(),
        P(),
    )
    return jax.shard_map(
        shards, mesh=mesh, in_specs=placed, out_specs=P("span", "ulysses", None), check_vma=False
    )
```

```python
import functools
import math

import jax
import jax.numpy as jnp
from jax import lax
from jax.experimental import pallas as pl
from jax.experimental.pallas import tpu as pltpu
from jax.sharding import PartitionSpec as P

MESH = pl.DeviceIdType.MESH
f32, bf16 = jnp.float32, jnp.bfloat16

HD = 128
TOK = 1536
OWN = 48
Z, Y, X = 8, 4, 4
WIDE = 6144
COLS = WIDE // 8
PASS = 3
PTOK = TOK // PASS
POWN = OWN // PASS
SLAB = Y * POWN
KC = 512
C = math.log2(math.e) / math.sqrt(HD)
LOW = -1e30
FIRST, LAST = slice(0, 4), slice(4, 8)


def remote(src, dst, send_sem, recv_sem, device):
    return pltpu.make_async_remote_copy(
        src_ref=src, dst_ref=dst, send_sem=send_sem, recv_sem=recv_sem, device_id=device, device_id_type=MESH
    )


def wait_bytes(ref, sem):
    pltpu.make_async_copy(ref, ref, sem).wait()


def aligned(index, size, multiple):
    return pl.ds(pl.multiple_of(index * size, multiple), size)


def kernel(
    q_in, k_in, v_in, w_in, gate_in, levels, first, out,
    qb, kb, vb, vt, st, po_r, ob, ag, wf, gt, gs, pb, hb, cb, yb, xb,
    a2a_s, a2a_r, kx_s, kx_r, vx_s, vx_r, qx_s, qx_r, po_ss, po_rs, oz_s, oz_r, ag_s, ag_r,
    wl, wp_s, wp_r, wm_s, wm_r, y_s, y_r, x_s, x_r,
):
    s, u = lax.axis_index("span"), lax.axis_index("ulysses")
    x, k = s // 2, s % 2
    z, y = u // Y, u % Y
    sib = x * 2 + (1 - k)
    my_cols = aligned(s, COLS, 128)

    barrier = pltpu.get_barrier_semaphore()

    def hail_ulysses(d, c):
        pl.semaphore_signal(barrier, inc=1, device_id=(s, (u + d) % 32), device_id_type=MESH)
        return c

    def hail_span(d, c):
        pl.semaphore_signal(barrier, inc=1, device_id=((s + d) % 8, u), device_id_type=MESH)
        return c

    lax.fori_loop(1, 32, hail_ulysses, 0)
    lax.fori_loop(1, 8, hail_span, 0)
    w_local = pltpu.make_async_copy(w_in.at[:, my_cols], wf.at[aligned(z, HD, 128)], wl.at[0])
    w_local.start()
    g_local = pltpu.make_async_copy(gate_in.at[:, my_cols], gt, wl.at[1])
    g_local.start()
    pl.semaphore_wait(barrier, 38)

    mine = aligned(u, OWN, 16)
    mine_q = aligned(u, POWN, 16)
    moves = (
        (lambda t: k_in.at[:, aligned(t, HD, 128)], kb.at[x, mine]),
        (lambda t: v_in.at[:, aligned(t, HD, 128)], vb.at[x, mine]),
        (lambda t: q_in.at[:, :, aligned(t, HD, 128)], qb.at[:, k, mine_q]),
    )
    for i, (src, dst) in enumerate(moves):

        def send_head(d, c, src=src, dst=dst, i=i):
            t = (u + d) % 32
            remote(src(t), dst, a2a_s.at[i], a2a_r.at[i], (s, t)).start()
            return c

        lax.fori_loop(1, 32, send_head, 0)
        pltpu.make_async_copy(src(u), dst, a2a_r.at[i]).start()

    pick = jnp.zeros((8, 64), f32)
    rows8 = lax.broadcasted_iota(jnp.int32, (8, 64), 0)
    cols64 = lax.broadcasted_iota(jnp.int32, (8, 64), 1)
    for c in range(8):
        pick = jnp.where((rows8 == c) & (cols64 == levels[c]), 1.0, pick)
    g_local.wait()
    gs[...] = jnp.dot(pick.astype(bf16), gt[...], preferred_element_type=f32)

    st[:, :, 0:HD] = jnp.zeros((PASS, 2, HD, PTOK), f32)
    st[:, :, HD : HD + 1] = jnp.full((PASS, 2, 1, PTOK), LOW, f32)
    st[:, :, HD + 1 : HD + 2] = jnp.zeros((PASS, 2, 1, PTOK), f32)

    def along(buf, sends, recvs, slot, i, chip, j):
        part = buf.at[slot, pl.ds(j * KC, KC)]
        return remote(part, part, sends.at[i, j], recvs.at[slot, j], (chip * 2 + k, u))

    k_sends = ((0, 0, 0, 1), (0, 0, 1, 3), (1, 1, 0, 2), (1, 1, 1, 0), (2, 2, 0, 3))
    k_relays = ((0, 1, 2, 3), (3, 0, 2, 2))
    v_sends = ((0, 0, 0, 1), (0, 0, 1, 3), (1, 1, 0, 2), (2, 2, 0, 3))
    v_relays = ((2, 1, 2, 3), (1, 0, 2, 2))
    chunks = TOK // KC
    drains = []

    def start_chunk(buf, sends, recvs, entry, j):
        at, slot, i, chip = entry
        copy = along(buf, sends, recvs, slot, i, chip, j)
        pl.when(x == at)(copy.start)
        drains.append(lambda: pl.when(x == at)(copy.wait_send))

    def arrived(buf, recvs, slot, j):
        wait_bytes(buf.at[slot, pl.ds(j * KC, KC)], recvs.at[slot, j])

    def exchange(buf, sends, recvs, direct, relays):
        for j in range(chunks):
            for entry in direct:
                start_chunk(buf, sends, recvs, entry, j)
        for j in range(chunks):
            for entry in relays:
                pl.when(x == entry[0])(functools.partial(arrived, buf, recvs, entry[1], j))
                start_chunk(buf, sends, recvs, entry, j)

    def await_rest(wanted):
        for at, buf, recvs, slot in wanted:

            @pl.when(x == at)
            def _():
                for j in range(chunks):
                    arrived(buf, recvs, slot, j)

    def turn(chip, c):
        vt[chip] = vb[chip].T
        return c

    wait_bytes(kb.at[x], a2a_r.at[0])
    exchange(kb, kx_s, kx_r, k_sends, k_relays)
    wait_bytes(vb.at[x], a2a_r.at[1])
    exchange(vb, vx_s, vx_r, v_sends, v_relays)
    turn(x, 0)
    def w_copies(t):
        up, down = (z + Z - t + 1) % Z, (z + t - 1) % Z
        size, shift = (HD, 0) if t < Z // 2 else (HD // 2, HD // 2)
        one = wf.at[pl.ds(pl.multiple_of(up * HD, 64), size)]
        two = wf.at[pl.ds(pl.multiple_of(down * HD + shift, 64), size)]
        i = t - 1
        return (
            remote(one, one, wp_s.at[i], wp_r.at[i], (s, (z + 1) % Z * Y + y)),
            remote(two, two, wm_s.at[i], wm_r.at[i], (s, (z + Z - 1) % Z * Y + y)),
        )

    def w_step(t):
        if t == 1:
            w_local.wait()
        else:
            for copy in w_copies(t - 1):
                copy.wait_recv()
        if t <= Z // 2:
            for copy in w_copies(t):
                copy.start()
                drains.append(copy.wait_send)


    w_step(1)

    wait_bytes(qb.at[:, k], a2a_r.at[2])
    q_send = remote(qb.at[:, k], qb.at[:, k], qx_s, qx_r, (sib, u))
    q_send.start()

    even, odd = first[x * 2], first[x * 2 + 1]

    def absorb(q, chip, seen, state):
        def scores(j):
            return lax.dot_general(
                kb[chip, pl.ds(j * KC, KC)], q, (((1,), (1,)), ((), ())), preferred_element_type=f32
            )

        now = scores(0)
        for j in range(chunks):
            later = scores(j + 1) if j + 1 < chunks else None
            top, total, accum = state
            new_top = jnp.maximum(top, jnp.where(seen, jnp.max(now, axis=0, keepdims=True), LOW))
            expo = jnp.exp2(now * C - jnp.where(seen, new_top * C, -LOW))
            shrink = jnp.exp2((top - new_top) * C)
            total = total * shrink + jnp.sum(expo, axis=0, keepdims=True)
            summed = jnp.dot(vt[chip, :, pl.ds(j * KC, KC)], expo.astype(bf16), preferred_element_type=f32)
            state = (new_top, total, accum * shrink + summed)
            now = later
        return state

    def load(p, w):
        return st[p, w, pl.ds(HD, 1)], st[p, w, pl.ds(HD + 1, 1)], st[p, w, pl.ds(0, HD)]

    def store(p, w, state):
        top, total, accum = state
        st[p, w, pl.ds(0, HD)] = accum
        st[p, w, pl.ds(HD, 1)] = top
        st[p, w, pl.ds(HD + 1, 1)] = total

    def pair(p, low, high):
        @pl.when(high >= low)
        def _():
            q = qb[p].reshape(2 * PTOK, HD)
            which = lax.broadcasted_iota(jnp.int32, (1, 2 * PTOK), 1) // PTOK
            start = jnp.where(which == 0, even, odd)

            def step(i, state):
                chip = high - i
                return absorb(q, chip, 2 * chip + k >= start, state)

            state = tuple(jnp.concatenate(pieces, axis=1) for pieces in zip(load(p, 0), load(p, 1)))
            state = lax.fori_loop(0, high - low + 1, step, state)
            for w in range(2):
                store(p, w, tuple(piece[:, w * PTOK : (w + 1) * PTOK] for piece in state))

    def single(p, w, start, low, high):
        @pl.when(high >= low)
        def _():
            q = qb[p, w]

            def step(i, state):
                chip = high - i
                return absorb(q, chip, 2 * chip + k >= start, state)

            store(p, w, lax.fori_loop(0, high - low + 1, step, load(p, w)))

    share = [remote(st.at[p, 1 - k], po_r.at[p], po_ss.at[p], po_rs.at[p], (sib, u)) for p in range(PASS)]

    def near(p):
        single(p, 1, odd, x, jnp.where(k == 1, x, x - 1))
        pair(p, jnp.maximum(x - 1, 0), x - k)

    def far(p):
        chip = jnp.where(x == 3, 1, 0)
        pair(p, chip, jnp.where((x == 2) | ((x == 3) & (k == 1)), chip, -1))
        pl.when(k == 0)(share[p].start)
        single(p, 0, even, 0, jnp.where(x == 3, 1 - k, -1))
        pl.when(k == 1)(share[p].start)
        drains.append(share[p].wait_send)

    def finish(p):
        wait_bytes(po_r.at[p], po_rs.at[p])
        top, total, accum = load(p, k)
        top2, total2 = po_r[p, HD : HD + 1], po_r[p, HD + 1 : HD + 2]
        both = jnp.maximum(top, top2)
        one_s = jnp.exp2((top - both) * C)
        two_s = jnp.exp2((top2 - both) * C)
        inv = 1.0 / (total * one_s + total2 * two_s)
        attn = accum * (one_s * inv) + po_r[p, 0:HD] * (two_s * inv)
        ob[p] = attn.astype(bf16).T
        there = ag.at[p, s, :, aligned(z, HD, 128)]

        def send_slab(d, c):
            t = (z + d) % Z
            remote(ob.at[p, aligned(t, SLAB, 16)], there, oz_s.at[p], oz_r.at[p], (s, t * Y + y)).start()
            return c

        lax.fori_loop(1, Z, send_slab, 0)
        pltpu.make_async_copy(ob.at[p, aligned(z, SLAB, 16)], there, oz_r.at[p]).start()
        drains.append(lambda: wait_bytes(ob.at[p, pl.ds(0, (Z - 1) * SLAB)], oz_s.at[p]))

    above, below = (y + 1) % Y, (y + Y - 1) % Y

    def start(copy):
        copy.start()
        drains.append(copy.wait_send)

    def ag_copy(p, slot, i, to):
        return remote(ag.at[p, slot], ag.at[p, slot], ag_s.at[p, i], ag_r.at[p, slot], (to, u))

    def gather(p):
        wait_bytes(ag.at[p, s], oz_r.at[p])
        for i, to in enumerate([((x + d) % X) * 2 + k for d in (2, 1, 3)] + [sib]):
            copy = ag_copy(p, s, i, to)
            copy.start()
            drains.append(copy.wait_send)

    def pass_on(p):
        for i, d in enumerate((1, 3, 2)):
            slot = ((x + d) % X) * 2 + k
            wait_bytes(ag.at[p, slot], ag_r.at[p, slot])
            copy = ag_copy(p, slot, 4 + i, sib)
            copy.start()
            drains.append(copy.wait_send)

    def project(p):
        for d in range(X):
            slot = ((x + d) % X) * 2 + 1 - k
            wait_bytes(ag.at[p, slot], ag_r.at[p, slot])
        part = jnp.dot(ag[p].reshape(8 * SLAB, Z * HD), wf[...], preferred_element_type=f32)
        pb[p] = part.astype(bf16).reshape(8, Y, POWN, COLS)
        for w, (t, far_spans, near_spans) in enumerate(((above, FIRST, LAST), (below, LAST, FIRST))):
            opposite = (y + 2) % Y
            start(remote(pb.at[p, far_spans, opposite], hb.at[p, w], y_s.at[p, w, 0], y_r.at[p, w, 0], (s, z * Y + t)))
            start(remote(pb.at[p, near_spans, t], yb.at[p, w, 1], y_s.at[p, w, 1], y_r.at[p, w, 1], (s, z * Y + t)))

    def forward(p):
        for w, (t, far_spans) in enumerate(((above, FIRST), (below, LAST))):
            wait_bytes(hb.at[p, w], y_r.at[p, w, 0])
            both = hb[p, w].astype(f32) + pb[p, far_spans, t].astype(f32)
            cb[p, w] = both.astype(bf16)
            start(remote(cb.at[p, w], yb.at[p, w, 0], y_s.at[p, w, 2], y_r.at[p, w, 2], (s, z * Y + t)))

    def settle(p):
        for w in range(2):
            wait_bytes(yb.at[p, w, 1], y_r.at[p, w, 1])
            wait_bytes(yb.at[p, w, 0], y_r.at[p, w, 2])
        for w, spans in enumerate((FIRST, LAST)):
            total = pb[p, spans, y].astype(f32) + yb[p, w, 0].astype(f32) + yb[p, 1 - w, 1].astype(f32)
            xb[p, spans] = (total * gs[spans].reshape(4, 1, COLS)).astype(bf16)
        there = out.at[pl.ds(p * POWN, POWN), my_cols]
        for i in range(1, 8):
            t = (s + i) % 8
            copy = remote(xb.at[p, t], there, x_s.at[p, i - 1], x_r.at[p], (t, u))
            copy.start()
            drains.append(copy.wait_send)
        pltpu.make_async_copy(xb.at[p, s], there, x_r.at[p]).start()

    await_rest(((1, kb, kx_r, 0), (2, kb, kx_r, 1), (3, kb, kx_r, 2), (3, vb, vx_r, 2)))
    lax.fori_loop(jnp.maximum(x - 1, 0), x, turn, 0)
    wait_bytes(qb.at[:, 1 - k], qx_r)

    def late():
        await_rest(
            ((2, kb, kx_r, 0), (2, vb, vx_r, 0), (3, vb, vx_r, 0), (3, kb, kx_r, 1), (3, vb, vx_r, 1))
        )
        lax.fori_loop(0, jnp.maximum(x - 1, 0), turn, 0)

    near(0)
    w_step(2)
    near(1)
    late()
    far(0)
    w_step(3)
    far(1)
    finish(0)
    near(2)
    w_step(4)
    finish(1)
    gather(0)
    far(2)
    gather(1)
    finish(2)
    pass_on(0)
    w_step(5)
    project(0)
    gather(2)
    pass_on(1)
    forward(0)
    project(1)
    pass_on(2)
    forward(1)
    project(2)
    settle(0)
    settle(1)
    forward(2)
    settle(2)
    for p in range(PASS):
        rows = out.at[pl.ds(p * POWN, POWN)]
        wait_bytes(rows, x_r.at[p])

    for i, buf in enumerate((kb.at[x], vb.at[x])):
        wait_bytes(buf.at[pl.ds(0, 31 * OWN)], a2a_s.at[i])
    wait_bytes(kb.at[x].at[pl.ds(0, 31 * OWN)], a2a_s.at[2])
    q_send.wait_send()
    for drain in drains:
        drain()


def shards(query, keys_in, values_in, out_weight, gate_table, levels, first_visible):
    anywhere = pl.BlockSpec(memory_space=pl.ANY)
    smem = pl.BlockSpec(memory_space=pltpu.SMEM)
    dma = pltpu.SemaphoreType.DMA
    vmem = pltpu.VMEM
    out = pl.pallas_call(
        kernel,
        out_shape=jax.ShapeDtypeStruct((OWN, WIDE), bf16),
        in_specs=[anywhere] * 5 + [smem, smem],
        out_specs=pl.BlockSpec(memory_space=pltpu.VMEM),
        scratch_shapes=[
            vmem((PASS, 2, PTOK, HD), bf16),
            vmem((X, TOK, HD), bf16),
            vmem((X, TOK, HD), bf16),
            vmem((X, HD, TOK), bf16),
            vmem((PASS, 2, HD + 8, PTOK), f32),
            vmem((PASS, HD + 8, PTOK), f32),
            vmem((PASS, PTOK, HD), bf16),
            vmem((PASS, 8, SLAB, Z * HD), bf16),
            vmem((Z * HD, COLS), bf16),
            vmem((64, COLS), bf16),
            vmem((8, COLS), f32),
            vmem((PASS, 8, Y, POWN, COLS), bf16),
            vmem((PASS, 2, 4, POWN, COLS), bf16),
            vmem((PASS, 2, 4, POWN, COLS), bf16),
            vmem((PASS, 2, 2, 4, POWN, COLS), bf16),
            vmem((PASS, 8, POWN, COLS), bf16),
            dma((3,)), dma((3,)),
            dma((3, 3)), dma((X, 3)), dma((3, 3)), dma((X, 3)),
            dma, dma,
            dma((PASS,)), dma((PASS,)),
            dma((PASS,)), dma((PASS,)),
            dma((PASS, 7)), dma((PASS, 8)),
            dma((2,)), dma((4,)), dma((4,)), dma((4,)), dma((4,)),
            dma((PASS, 2, 3)), dma((PASS, 2, 3)),
            dma((PASS, 7)), dma((PASS,)),
        ],
        compiler_params=pltpu.CompilerParams(
            collective_id=0, has_side_effects=True, vmem_limit_bytes=56 * 2**20
        ),
    )(
        query.reshape(PASS, POWN, query.shape[2]), keys_in[0], values_in[0], out_weight, gate_table, levels,
        first_visible,
    )
    return out[None]


def solution(mesh):
    placed = (
        P("span", "ulysses", None),
        P("span", "ulysses", None),
        P("span", "ulysses", None),
        P("ulysses", None),
        P(),
        P(),
        P(),
    )
    return jax.shard_map(
        shards, mesh=mesh, in_specs=placed, out_specs=P("span", "ulysses", None), check_vma=False
    )
```
